256 devices in a mesh: section: 64 (over y_lo, z, x), tensor: 4 (over y_hi, core).
Axes of the slice: x: 4, y: 4 (y_hi: 2, y_lo: 2; y = y_hi * 2 + y_lo), z: 8, core: 2. Of those that a mesh axis runs over, the one named last changes fastest.
Arguments:
- acts: bfloat16 [64, 512, 4096], P('section', 'tensor'), may hold values from -6 to 6
- norm_gain: float32 [64, 4096], P('section'), may hold values from 0.1 to 1.9
- w_qkv: bfloat16 [64, 4096, 3072], P('section', None, 'tensor'), may hold values from -0.09375 to 0.09375
- w_out: bfloat16 [64, 2048, 4096], P('section', 'tensor'), may hold values from -0.75 to 0.75
- kv_cache: bfloat16 [64, 1024, 1024], P('section', None, 'tensor')
- block_index: int32 [64], P('section'), may hold values from 0 to 63, as said below
- valid_len: int32 [64], P('section'), may hold values from 0 to 1024, as said below
Outputs:
- passed: bfloat16 [64, 512, 4096], P('section', 'tensor')
The draws below stay inside these ranges and needn't reach their ends.
Inputs may be any that keep to these rules, and one draw needn't show every extreme that they name: `block_index`: some section holds block 0 and some the last block of the prompt. `valid_len`: some section has no live cached positions and some has all.
All inputs are finite; a program needn't handle non-finite values.
Results may differ from the reference program's by a relative error of at most 0.029.
Values may be sent and summed in bfloat16 or wider, within the bound.
A program may use at most 128 MiB of HBM per device.

```python
import math
import jax
import jax.numpy as jnp
from jax import lax

D = 4096
HD = 128
GROUP = 4
BLOCK = 512
CACHE_LEN = 1024
PROMPT = 32768
KV_HEADS = 4
SECTIONS = 64
N_SECTION = 64


def draw_kv_cache(key, part):
    key = jax.random.fold_in(key, 11)
    keys_split = jax.random.split(key, 1)
    shape = (N_SECTION, CACHE_LEN, 2 * KV_HEADS * HD)
    normal_part = jax.random.normal(keys_split[0], shape, jnp.float32)
    result = normal_part
    return result.astype(jnp.bfloat16)


def ends_forced(key, limit):
    keys_split = jax.random.split(key, 2)
    drawn = jax.random.randint(keys_split[0], (N_SECTION,), 0, limit + 1, jnp.int32)
    order = jax.random.permutation(keys_split[1], N_SECTION)
    drawn = drawn.at[order[0]].set(limit)
    return drawn.at[order[1]].set(0)


def draw_block_index(key, part):
    key = jax.random.fold_in(key, 21)
    return ends_forced(key, PROMPT // BLOCK - 1)


def draw_valid_len(key, part):
    key = jax.random.fold_in(key, 31)
    return ends_forced(key, CACHE_LEN)


def block_scale(key, extent, cuts, least, high):
    level = 1.0
    for dim, shards_of in cuts:
        draws = jax.random.uniform(jax.random.fold_in(jax.random.fold_in(key, 6), dim), (shards_of,), jnp.float32, least / len(cuts), high / len(cuts))
        level = level * jnp.repeat(jnp.exp(draws), extent[dim] // shards_of).reshape((-1,) + (1,) * (len(extent) - 1 - dim))
    return level


def scatter_about(key, dims, width, most, cuts=(), held_as=jnp.bfloat16):
    array = jax.random.normal(key, dims, jnp.float32) * width
    if len(cuts) > 0:
        array = block_scale(key, dims, cuts, -0.22, 0.18) * array
    return jnp.clip(array, min=-most, max=most).astype(held_as)


def setup_inputs(seed: int = 0) -> dict:
    keys = jax.random.split(jax.random.key(seed), 8)
    return {
        "acts": scatter_about(keys[0], (SECTIONS, BLOCK, D), 1.0, 6.0, ((0, 64), (1, 4))),
        "norm_gain": jnp.clip(1.0 + 0.18 * jax.random.normal(keys[1], (SECTIONS, D), jnp.float32), 0.1, 1.9),
        "w_qkv": scatter_about(keys[2], (SECTIONS, D, KV_HEADS * (GROUP + 2) * HD), D ** -0.5, 0.09375, ((0, 64), (2, 4))),
        "w_out": scatter_about(keys[3], (SECTIONS, KV_HEADS * GROUP * HD, D), (GROUP * HD // 8) ** -0.5, 0.75, ((0, 64), (1, 4))),
        "kv_cache": draw_kv_cache(jax.random.fold_in(keys[7], 71), 0),
        "block_index": draw_block_index(jax.random.fold_in(keys[7], 71), 0),
        "valid_len": draw_valid_len(jax.random.fold_in(keys[7], 71), 0),
    }


def rotate(table, positions):
    half_dim = table.shape[-1] // 2
    inv_freq = jnp.exp(-jnp.log(jnp.float32(500000.0)) * (2.0 * jnp.arange(half_dim, dtype=jnp.float32) / (2 * half_dim)))
    angles = positions.astype(jnp.float32)[:, None] * inv_freq[None, :]
    shape = (table.shape[0],) + (1,) * (table.ndim - 2) + (half_dim,)
    cosine = jnp.cos(angles).reshape(shape)
    sine = jnp.sin(angles).reshape(shape)
    first = table[..., :half_dim]
    second = table[..., half_dim:]
    return jnp.concatenate([first * cosine - second * sine, second * cosine + first * sine], -1)

def section_step(tok_rows, gain, weight_in, weight_out, stored, index, valid):
    residual = tok_rows.astype(jnp.float32)
    normed = (residual * lax.rsqrt(lax.optimization_barrier(jnp.mean(residual * residual, -1, keepdims=True)) + 1e-05) * gain[None, :]).astype(jnp.bfloat16)
    qkv = jnp.dot(normed, weight_in, preferred_element_type=jnp.float32).reshape(BLOCK, -1, GROUP + 2, HD)
    positions = index.astype(jnp.int32) * BLOCK + jnp.arange(BLOCK, dtype=jnp.int32)
    queries = rotate(qkv[:, :, :GROUP], positions).astype(jnp.bfloat16)
    new_keys = rotate(qkv[:, :, GROUP], positions).astype(jnp.bfloat16)
    new_values = qkv[:, :, GROUP + 1].astype(jnp.bfloat16)
    cached = stored.reshape(CACHE_LEN, -1, 2, HD)
    score_scale = 1.0 / math.sqrt(HD)
    s_cache = jnp.einsum('qhgd,khd->hgqk', queries.astype(jnp.float32), cached[:, :, 0].astype(jnp.float32)) * score_scale
    live_mask = (jnp.arange(CACHE_LEN, dtype=jnp.int32) < valid)[None, None, None, :]
    s_cache = jnp.where(live_mask, s_cache, -jnp.inf)
    s_own = jnp.einsum('qhgd,khd->hgqk', queries.astype(jnp.float32), new_keys.astype(jnp.float32)) * score_scale
    causal = (jnp.arange(BLOCK)[:, None] >= jnp.arange(BLOCK)[None, :])[None, None]
    s_own = jnp.where(causal, s_own, -jnp.inf)
    row_max = jnp.maximum(lax.optimization_barrier(jnp.max(s_cache, -1, keepdims=True)), lax.optimization_barrier(jnp.max(s_own, -1, keepdims=True)))
    e_cache = jnp.exp(s_cache - row_max)
    e_own = jnp.exp(s_own - row_max)
    softmax_total = lax.optimization_barrier(jnp.sum(e_cache, -1, keepdims=True)) + lax.optimization_barrier(jnp.sum(e_own, -1, keepdims=True))
    p_cache = (e_cache / softmax_total).astype(jnp.bfloat16)
    p_own = (e_own / softmax_total).astype(jnp.bfloat16)
    attn = jnp.einsum('hgqk,khd->qhgd', p_cache.astype(jnp.float32), cached[:, :, 1].astype(jnp.float32))
    attn = attn + jnp.einsum('hgqk,khd->qhgd', p_own.astype(jnp.float32), new_values.astype(jnp.float32))
    attn = attn.astype(jnp.bfloat16).reshape(BLOCK, -1)
    delta = jnp.dot(attn, weight_out, preferred_element_type=jnp.float32)
    return (residual + delta).astype(jnp.bfloat16)

def reference(acts, norm_gain, w_qkv, w_out, kv_cache, block_index, valid_len):
    updated = lax.map(lambda items: section_step(*items), (acts, norm_gain, w_qkv, w_out, kv_cache, block_index, valid_len))
    return jnp.roll(updated, 1, axis=0)
```

```python
import functools
import math

import jax
import jax.numpy as jnp
import numpy as np
from jax import lax
from jax.experimental import pallas as pl
from jax.experimental.pallas import tpu as pltpu
from jax.sharding import PartitionSpec as P

GROUP = 4
HD = 128
AG = 4
PIECE = 16
MESH = pl.DeviceIdType.MESH
F32 = jnp.float32
BF16 = jnp.bfloat16


def kernel(
    sections, bidx, vlen, freq, acts, gain, wqkv, wout, cache, out,
    a_v, g_v, nrm, wq, wo, kv, bias, ct, st, qb, kb, vb, att, res, base, snd, rcv, bsnd, brcv, fin,
    l_sem, ag_s, ag_r, mt_s, mt_r, fw_s, fw_r, wo_s, wo_r, at_s, at_r, rs_s, rs_r, bs_s, bs_r, x_s, x_r,
):
    rows, dim = a_v.shape
    wide = dim // 2
    chunk = rows // AG
    part_rows = rows // 2
    per = part_rows // PIECE
    half = sections // 2

    s = lax.axis_index("section")
    t = lax.axis_index("tensor")
    c = lax.rem(t, 2)
    hi = lax.div(t, 2)
    low = lax.rem(s, half)
    last = lax.div(low, half - 1)
    nxt = s - low + lax.rem(low + 1, half)
    prv = s - low + lax.rem(low + half - 1, half)
    oth = lax.rem(s + half, sections)
    mate = (s, 2 * hi + 1 - c)
    partner = (s, 2 * (1 - hi) + c)
    sum_dev = (lax.rem(s + half * last, sections), 2 * (1 - hi) + c)
    base_dev = (oth, t)
    special = last == 1

    def remote(src, dst, ss, rs, dev):
        return pltpu.make_async_remote_copy(
            src_ref=src, dst_ref=dst, send_sem=ss, recv_sem=rs, device_id=dev, device_id_type=MESH
        )

    mine = pl.ds(pl.multiple_of(c * wide, wide), wide)
    others = pl.ds(pl.multiple_of((1 - c) * wide, wide), wide)
    g_cp = pltpu.make_async_copy(gain, g_v, l_sem.at[AG])
    a_cp = [
        pltpu.make_async_copy(
            acts.at[0, pl.ds(j * chunk, chunk)], a_v.at[pl.ds(j * chunk, chunk)], l_sem.at[j]
        )
        for j in range(AG)
    ]
    a_cp[0].start()
    g_cp.start()
    for j in range(1, AG):
        a_cp[j].start()
    wq_cp = pltpu.make_async_copy(wqkv.at[0], wq, l_sem.at[AG + 1])
    kv_cp = pltpu.make_async_copy(cache.at[0], kv, l_sem.at[AG + 2])
    wo_cp = pltpu.make_async_copy(wout.at[0, :, mine], wo.at[0], l_sem.at[AG + 3])
    res_cp = pltpu.make_async_copy(acts.at[0, :, mine], res.at[c], l_sem.at[AG + 4])
    wq_cp.start()
    kv_cp.start()

    barrier = pltpu.get_barrier_semaphore()
    for dev in (
        partner, mate, (nxt, 2 * hi), (nxt, 2 * hi + 1), (prv, 2 * hi), (prv, 2 * hi + 1),
    ):
        pl.semaphore_signal(barrier, inc=1, device_id=dev, device_id_type=MESH)

    @pl.when(special)
    def _():
        for dev in (base_dev, sum_dev):
            pl.semaphore_signal(barrier, inc=1, device_id=dev, device_id_type=MESH)

    def ag_copy(j):
        r = pl.ds(j * chunk, chunk)
        return remote(nrm.at[c, r], nrm.at[2 + c, r], ag_s.at[j], ag_r.at[j], partner)

    def mate_copy(j):
        r = pl.ds(j * chunk, chunk)
        return remote(nrm.at[c, r], nrm.at[c, r], mt_s.at[j], mt_r.at[j], mate)

    def mate_arrival(j):
        r = pl.ds(j * chunk, chunk)
        return remote(nrm.at[1 - c, r], nrm.at[1 - c, r], mt_s.at[j], mt_r.at[j], mate)

    def fwd_copy(j):
        r = pl.ds(j * chunk, chunk)
        return remote(nrm.at[2 + c, r], nrm.at[2 + c, r], fw_s.at[j], fw_r.at[j], mate)

    def fwd_arrival(j):
        r = pl.ds(j * chunk, chunk)
        return remote(nrm.at[3 - c, r], nrm.at[3 - c, r], fw_s.at[j], fw_r.at[j], mate)

    def normalize(j):
        a_cp[j].wait()
        r = pl.ds(j * chunk, chunk)
        x = a_v[r, :].astype(F32)
        ms = jnp.mean(x * x, -1, keepdims=True)
        nrm[c, r, :] = (x * lax.rsqrt(ms + 1e-05) * g_v[...]).astype(BF16)

    g_cp.wait()
    normalize(0)
    pl.semaphore_wait(barrier, 6 + 2 * last)

    ag_copy(0).start()
    mate_copy(0).start()
    for j in range(1, AG):
        normalize(j)
        ag_copy(j).start()
        mate_copy(j).start()

    wo_cp.start()
    res_cp.start()
    wo_rm = remote(wout.at[0, :, others], wo.at[1], wo_s.at[0], wo_r.at[0], mate)
    res_rm = remote(acts.at[0, :, others], res.at[c], wo_s.at[1], wo_r.at[1], mate)
    res_in = remote(acts.at[0, :, mine], res.at[1 - c], wo_s.at[1], wo_r.at[1], mate)
    wo_rm.start()
    res_rm.start()

    kb[...] = jnp.zeros_like(kb)
    vb[...] = jnp.zeros_like(vb)
    lane = lax.broadcasted_iota(jnp.int32, (rows, HD), 1)
    sign = jnp.where(lane < HD // 2, -1.0, 1.0).astype(F32)
    row = lax.broadcasted_iota(jnp.int32, (rows, HD), 0)

    def tables(k, _):
        rel, b = lax.div(k, 2), lax.rem(k, 2)
        side = hi + rel - 2 * hi * rel
        pos = bidx[0] * (4 * rows) + (2 * side + b) * rows + row
        angle = pos.astype(F32) * freq[...]
        turns = jnp.floor(angle * np.float32(1.0 / (2.0 * math.pi)) + 0.5)
        small = ((angle - turns * TURN[0]) - turns * TURN[1]) - turns * TURN[2]
        r = pl.ds(pl.multiple_of(k * rows, rows), rows)
        ct[r, :] = jnp.cos(small)
        st[r, :] = jnp.sin(small) * sign
        return 0

    lax.fori_loop(0, 4, tables, 0)
    key_id = lax.broadcasted_iota(jnp.int32, bias.shape, 1)
    bias[...] = jnp.where(key_id < vlen[0], 0.0, -jnp.inf).astype(F32)

    def project(rel, h):
        x = nrm[2 * rel : 2 * rel + 2, pl.ds(pl.multiple_of(h * part_rows, part_rows), part_rows), :]
        x = x.reshape(2 * part_rows, dim)

        def tab(ref, b):
            off = pl.multiple_of((2 * rel + b) * rows + h * part_rows, part_rows)
            return ref[pl.ds(off, part_rows), :]

        def turned(v, b):
            return (v * tab(ct, b) + pltpu.roll(v, HD // 2, 1) * tab(st, b)).astype(BF16)

        for n in range(3):
            y = jnp.dot(x, wq[:, 2 * n * HD : 2 * (n + 1) * HD], preferred_element_type=F32)
            for b in range(2):
                yb = y[b * part_rows : (b + 1) * part_rows]
                if n < 2:
                    for k in range(2):
                        at = (2 * n + k) * part_rows
                        qb[rel, b, h, at : at + part_rows, :] = turned(yb[:, k * HD : (k + 1) * HD], b)
                else:
                    off = pl.multiple_of((2 * rel + b) * rows + h * part_rows, part_rows)
                    kb[pl.ds(off, part_rows), :] = turned(yb[:, :HD], b)
                    vb[pl.ds(off, part_rows), :] = yb[:, HD:].astype(BF16)

    factor = np.float32(math.log2(math.e) / math.sqrt(HD))

    def att_copy(rel, r):
        k = 4 * rel + r
        return remote(att.at[0, rel, r], att.at[1, rel, r], at_s.at[k], at_r.at[k], mate)

    def attend(rel, r):
        b, h = r // 2 if isinstance(r, int) else lax.div(r, 2), r % 2 if isinstance(r, int) else lax.rem(r, 2)
        side = 1 - hi if rel else hi
        q = qb[rel, b, h]
        nt = (((1,), (1,)), ((), ()))
        sc = lax.dot_general(q, kv[:, :HD], nt, preferred_element_type=F32) + bias[...]
        sn = lax.dot_general(q, kb[...], nt, preferred_element_type=F32)
        kid = lax.broadcasted_iota(jnp.int32, (1, 4 * rows), 1)
        kpos = jnp.where(kid < 2 * rows, kid + 2 * rows * hi, kid - 2 * rows * hi)
        qid = lax.rem(lax.broadcasted_iota(jnp.int32, (GROUP * part_rows, 1), 0), part_rows)
        qpos = qid + (2 * rows * side + rows * b + part_rows * h)
        sn = jnp.where(kpos <= qpos, sn, -jnp.inf)
        m = jnp.maximum(jnp.max(sc, -1, keepdims=True), jnp.max(sn, -1, keepdims=True))
        ec = jnp.exp2((sc - m) * factor)
        en = jnp.exp2((sn - m) * factor)
        total = jnp.sum(ec, -1, keepdims=True) + jnp.sum(en, -1, keepdims=True)
        o = jnp.dot(ec.astype(BF16), kv[:, HD:], preferred_element_type=F32)
        o = o + jnp.dot(en.astype(BF16), vb[...], preferred_element_type=F32)
        o = (o / total).astype(BF16)
        for k in range(GROUP):
            att[0, rel, r, :, k * HD : (k + 1) * HD] = o[k * part_rows : (k + 1) * part_rows]
        att_copy(rel, r).start()

    tile = wide // 4

    def output(rel, r):
        att_copy(rel, r).wait_recv()
        at = pl.ds(pl.multiple_of(r * part_rows, part_rows), part_rows)
        b, h = lax.div(r, 2), lax.rem(r, 2)
        inner = pl.ds(pl.multiple_of(h * part_rows, part_rows), part_rows)
        for n in range(4):
            cols = slice(n * tile, (n + 1) * tile)
            y = jnp.dot(att[0, rel, r], wo[0, :, cols], preferred_element_type=F32)
            y = y + jnp.dot(att[1, rel, r], wo[1, :, cols], preferred_element_type=F32)
            if rel:
                snd[at, cols] = y.astype(BF16)
            else:
                y = y + res[b, inner, cols].astype(F32)
                base[at, cols] = y

                @pl.when(special)
                def _():
                    bsnd[at, cols] = y.astype(BF16)

        if rel:
            for i in range(per):
                sum_copy(r * per + i).start()
        else:

            @pl.when(special)
            def _():
                base_copy(r).start()

    def piece(f):
        return pl.ds(pl.multiple_of(f * PIECE, PIECE), PIECE)

    def sum_copy(f):
        return remote(snd.at[piece(f)], rcv.at[piece(f)], rs_s.at[f], rs_r.at[f], sum_dev)

    def base_copy(r):
        at = pl.ds(pl.multiple_of(r * part_rows, part_rows), part_rows)
        return remote(bsnd.at[at], brcv.at[at], bs_s.at[r], bs_r.at[r], base_dev)

    in_block = 2 * per

    def x_copy(f):
        b, k = lax.div(f, in_block), lax.rem(f, in_block)
        return remote(
            fin.at[piece(f)], out.at[0, piece(k), mine], x_s.at[f], x_r.at[c * in_block + k], (nxt, 2 * hi + b)
        )

    def finish(f):
        sum_copy(f).wait_recv()

        @pl.when(special)
        def _():
            @pl.when(lax.rem(f, per) == 0)
            def _():
                base_copy(lax.div(f, per)).wait_recv()

            fin[piece(f), :] = (brcv[piece(f), :].astype(F32) + rcv[piece(f), :].astype(F32)).astype(BF16)

        @pl.when(jnp.logical_not(special))
        def _():
            fin[piece(f), :] = (base[piece(f), :] + rcv[piece(f), :].astype(F32)).astype(BF16)

        x_copy(f).start()

    for j in range(AG):
        mate_arrival(j).wait_recv()
    wq_cp.wait()

    def own_projection(h, _):
        project(0, h)
        return 0

    lax.fori_loop(0, 2, own_projection, 0)
    kv_cp.wait()

    for j in range(AG // 2):
        ag_copy(j).wait_recv()
        fwd_copy(j).start()
    for j in range(AG // 2):
        fwd_arrival(j).wait_recv()
    project(1, 0)
    attend(1, 0)
    wo_cp.wait()
    wo_rm.wait_recv()
    res_cp.wait()
    res_in.wait_recv()
    output(1, 0)

    for j in range(AG // 2, AG):
        ag_copy(j).wait_recv()
        fwd_copy(j).start()
    for j in range(AG // 2, AG):
        fwd_arrival(j).wait_recv()
    project(1, 1)

    def step(r, _):
        attend(0, r)
        attend(1, r + 1)
        output(0, r)
        finish(2 * r)
        finish(2 * r + 1)
        output(1, r + 1)
        return 0

    lax.fori_loop(0, 3, step, 0)
    attend(0, 3)
    output(0, 3)

    def tail(f, _):
        finish(f)
        return 0

    lax.fori_loop(6, 4 * per, tail, 0)

    for j in range(AG):
        ag_copy(j).wait_send()
        mate_copy(j).wait_send()
        fwd_copy(j).wait_send()
    wo_rm.wait_send()
    res_rm.wait_send()

    def drain_att(k, _):
        remote(att.at[0, 0, 0], att.at[1, 0, 0], at_s.at[k], at_r.at[k], mate).wait_send()
        return 0

    lax.fori_loop(0, 8, drain_att, 0)

    def drain(f, _):
        sum_copy(f).wait_send()
        x_copy(f).wait_send()
        return 0

    lax.fori_loop(0, 4 * per, drain, 0)

    @pl.when(special)
    def _():
        def drain_base(r, _):
            base_copy(r).wait_send()
            return 0

        lax.fori_loop(0, 4, drain_base, 0)

    def arrive(k, _):
        side, f = lax.div(k, in_block), lax.rem(k, in_block)
        cols = pl.ds(pl.multiple_of(side * wide, wide), wide)
        remote(fin.at[piece(f)], out.at[0, piece(f), cols], x_s.at[k], x_r.at[k], mate).wait_recv()
        return 0

    lax.fori_loop(0, 2 * in_block, arrive, 0)


def split_turn():
    whole, parts = 2.0 * math.pi, []
    for _ in range(2):
        scale = 2.0 ** (math.frexp(whole)[1] - 10)
        part = math.floor(whole / scale) * scale
        parts.append(np.float32(part))
        whole -= part
    return (*parts, np.float32(whole))


TURN = split_turn()


def body(sections, acts, norm_gain, w_qkv, w_out, kv_cache, block_index, valid_len):
    rows, dim = acts.shape[1:]
    wide = dim // 2
    cached = kv_cache.shape[1]
    width = w_qkv.shape[2]
    heads = w_out.shape[1]
    exponent = 2.0 * (np.arange(HD) % (HD // 2)) / HD
    freq = jnp.asarray(np.exp(-np.log(500000.0) * exponent).astype(np.float32)[None])
    step = rows // 2
    pieces = 2 * rows // PIECE
    dma = pltpu.SemaphoreType.DMA
    smem = pl.BlockSpec(memory_space=pltpu.SMEM)
    hbm = pl.BlockSpec(memory_space=pl.ANY)
    return pl.pallas_call(
        functools.partial(kernel, sections),
        out_shape=jax.ShapeDtypeStruct((1, rows, dim), BF16),
        in_specs=[smem, smem, pl.BlockSpec(memory_space=pltpu.VMEM)] + [hbm] * 5,
        out_specs=hbm,
        scratch_shapes=[
            pltpu.VMEM((rows, dim), BF16),
            pltpu.VMEM((1, dim), F32),
            pltpu.VMEM((4, rows, dim), BF16),
            pltpu.VMEM((dim, width), BF16),
            pltpu.VMEM((2, heads, wide), BF16),
            pltpu.VMEM((cached, 2 * HD), BF16),
            pltpu.VMEM((1, cached), F32),
            pltpu.VMEM((4 * rows, HD), F32),
            pltpu.VMEM((4 * rows, HD), F32),
            pltpu.VMEM((2, 2, 2, GROUP * step, HD), BF16),
            pltpu.VMEM((4 * rows, HD), BF16),
            pltpu.VMEM((4 * rows, HD), BF16),
            pltpu.VMEM((2, 2, 4, step, heads), BF16),
            pltpu.VMEM((2, rows, wide), BF16),
            pltpu.VMEM((2 * rows, wide), F32),
            pltpu.VMEM((2 * rows, wide), BF16),
            pltpu.VMEM((2 * rows, wide), BF16),
            pltpu.VMEM((2 * rows, wide), BF16),
            pltpu.VMEM((2 * rows, wide), BF16),
            pltpu.VMEM((2 * rows, wide), BF16),
            dma((AG + 5,)),
            dma((AG,)), dma((AG,)), dma((AG,)), dma((AG,)), dma((AG,)), dma((AG,)),
            dma((2,)), dma((2,)), dma((8,)), dma((8,)),
            dma((pieces,)), dma((pieces,)), dma((4,)), dma((4,)), dma((pieces,)), dma((pieces,)),
        ],
        compiler_params=pltpu.CompilerParams(
            collective_id=0, has_side_effects=True, vmem_limit_bytes=56 * 2**20
        ),
    )(block_index, valid_len, freq, acts, norm_gain, w_qkv, w_out, kv_cache)


def solution(mesh):
    in_specs = (
        P("section", "tensor", None),
        P("section", None),
        P("section", None, "tensor"),
        P("section", "tensor", None),
        P("section", None, "tensor"),
        P("section"),
        P("section"),
    )
    out_specs = P("section", "tensor", None)
    return jax.shard_map(
        functools.partial(body, mesh.shape["section"]),
        mesh=mesh, in_specs=in_specs, out_specs=out_specs, check_vma=False,
    )
```

```python
import functools
import math

import jax
import jax.numpy as jnp
import numpy as np
from jax import lax
from jax.experimental import pallas as pl
from jax.experimental.pallas import tpu as pltpu
from jax.sharding import PartitionSpec as P

HELPERS = (30, 28, 27, 3)
GROUP = 4
HD = 128
AG = 4
PIECE = 16
MESH = pl.DeviceIdType.MESH
F32 = jnp.float32
BF16 = jnp.bfloat16


def kernel(
    sections, bidx_in, vlen_in, freq_in, acts, gain, wqkv, wout, cache, out,
    bidx, vlen, freq, a_v, g_v, nrm, wq, wo, kall, vall, bias, ct, st, qb, acc, top, total, att, res, base, snd, rcv, bsnd, brcv, fin, relay,
    l_sem, ag_s, ag_r, mt_s, mt_r, fw_s, fw_r, wo_s, wo_r, at_s, at_r, rs_s, rs_r, bs_s, bs_r, x_s, x_r, ro_s, ro_r, ri_s, ri_r,
):
    rows, dim = a_v.shape
    wide = dim // 2
    chunk = rows // AG
    part = rows // 2
    per = part // PIECE
    half = sections // 2
    cached = cache.shape[1]
    heads = wout.shape[1]
    pieces = 4 * per

    s = lax.axis_index("section")
    t = lax.axis_index("tensor")
    c = lax.rem(t, 2)
    hi = lax.div(t, 2)
    low = lax.rem(s, half)
    last = lax.div(low, half - 1)
    nxt = s - low + lax.rem(low + 1, half)
    prv = s - low + lax.rem(low + half - 1, half)
    oth = lax.rem(s + half, sections)
    mate = (s, 2 * hi + 1 - c)
    partner = (s, 2 * (1 - hi) + c)
    sum_dev = (lax.rem(s + half * last, sections), 2 * (1 - hi) + c)
    base_dev = (oth, t)
    first = s - low
    ends = first + half - 1
    helper = [low == k for k in HELPERS]
    relays = functools.reduce(jnp.logical_or, helper)
    quarter = sum(jnp.where(helper[q], q, 0) for q in range(1, len(HELPERS)))
    cross_dev = (oth, 2 * (1 - hi) + c)
    special = last == 1

    def remote(src, dst, ss, rs, dev):
        return pltpu.make_async_remote_copy(
            src_ref=src, dst_ref=dst, send_sem=ss, recv_sem=rs, device_id=dev, device_id_type=MESH
        )

    def span(start, size):
        return pl.ds(pl.multiple_of(start, size), size)

    mine = span(c * wide, wide)
    others = span((1 - c) * wide, wide)
    g_cp = pltpu.make_async_copy(gain, g_v, l_sem.at[AG])
    a_cp = [
        pltpu.make_async_copy(
            acts.at[0, pl.ds(j * chunk, chunk)], a_v.at[pl.ds(j * chunk, chunk)], l_sem.at[j]
        )
        for j in range(AG)
    ]
    a_cp[0].start()
    g_cp.start()
    small = [
        pltpu.make_async_copy(src, dst, l_sem.at[AG + 6 + i])
        for i, (src, dst) in enumerate(((bidx_in, bidx), (vlen_in, vlen), (freq_in, freq)))
    ]
    for j in range(1, AG):
        a_cp[j].start()

    barrier = pltpu.get_barrier_semaphore()
    for dev in (partner, mate, (prv, 2 * hi), (prv, 2 * hi + 1)):
        pl.semaphore_signal(barrier, inc=1, device_id=dev, device_id_type=MESH)

    @pl.when(special)
    def _():
        for dev in (base_dev, cross_dev, *[(first + k, t) for k in HELPERS]):
            pl.semaphore_signal(barrier, inc=1, device_id=dev, device_id_type=MESH)

    @pl.when(relays)
    def _():
        pl.semaphore_signal(barrier, inc=1, device_id=(ends, 2 * (1 - hi) + c), device_id_type=MESH)

    wq_cp = pltpu.make_async_copy(wqkv.at[0], wq, l_sem.at[AG + 1])
    k_cp = pltpu.make_async_copy(cache.at[0, :, :HD], kall.at[:cached], l_sem.at[AG + 2])
    v_cp = pltpu.make_async_copy(cache.at[0, :, HD:], vall.at[:cached], l_sem.at[AG + 3])
    wo_cp = pltpu.make_async_copy(wout.at[0, :, mine], wo.at[:heads], l_sem.at[AG + 4])
    res_cp = pltpu.make_async_copy(acts.at[0, :, mine], res.at[c], l_sem.at[AG + 5])
    wq_cp.start()
    k_cp.start()
    v_cp.start()
    for cp in small:
        cp.start()

    def ag_copy(j):
        r = span((2 * (j % 2) + c) * chunk, chunk)
        return remote(nrm.at[j // 2, r], nrm.at[2 + j // 2, r], ag_s.at[j], ag_r.at[j], partner)

    def mate_copy(k):
        r = span(k * chunk, chunk)
        return remote(nrm.at[c, r], nrm.at[c, r], mt_s.at[k], mt_r.at[k], mate)

    def mate_arrival(k):
        r = span(k * chunk, chunk)
        return remote(nrm.at[1 - c, r], nrm.at[1 - c, r], mt_s.at[k], mt_r.at[k], mate)

    def passed_on(j, core):
        slot, r = 2 + lax.div(j, 2), span((2 * lax.rem(j, 2) + core) * chunk, chunk)
        return remote(nrm.at[slot, r], nrm.at[slot, r], fw_s.at[j], fw_r.at[j], mate)

    def arrived(j):
        slot, r = 2 + lax.div(j, 2), span((2 * lax.rem(j, 2) + c) * chunk, chunk)
        return remote(nrm.at[slot, r], nrm.at[slot, r], ag_s.at[j], ag_r.at[j], partner)

    qw = dim // len(HELPERS)
    late = span((2 + c) * chunk, chunk)

    def relay_out(q):
        return remote(
            nrm.at[1, late, pl.ds(q * qw, qw)], relay, ro_s.at[q], ro_r.at[0],
            (first + HELPERS[q], 2 * (1 - hi) + c),
        )

    def relay_in():
        return remote(relay, nrm.at[3, late, span(quarter * qw, qw)], ri_s.at[0], ri_r.at[quarter], (ends, t))

    def relay_arrival(q):
        return remote(relay, nrm.at[3, late, pl.ds(q * qw, qw)], ri_s.at[0], ri_r.at[q], mate)

    g_cp.wait()
    for j in range(AG):
        a_cp[j].wait()
        r = pl.ds(j * chunk, chunk)
        x = a_v[r, :].astype(F32)
        ms = jnp.mean(x * x, -1, keepdims=True)
        nrm[c, r, :] = (x * lax.rsqrt(ms + 1e-05) * g_v[...]).astype(BF16)

    pl.semaphore_wait(barrier, 4 + (2 + len(HELPERS)) * last + jnp.where(relays, 1, 0))

    @pl.when(c == 0)
    def _():
        ag_copy(0).start()
        ag_copy(1).start()

    mate_copy(1 - c).start()
    mate_copy(3 - c).start()
    mate_arrival(c).wait_recv()
    mate_arrival(c + 2).wait_recv()

    @pl.when(c == 1)
    def _():
        ag_copy(0).start()
        ag_copy(1).start()

    ag_copy(2).start()

    @pl.when(special)
    def _():
        for q in range(len(HELPERS)):
            relay_out(q).start()

    @pl.when(jnp.logical_not(special))
    def _():
        ag_copy(3).start()

    mate_copy(c).start()
    mate_copy(c + 2).start()

    wo_cp.start()
    res_cp.start()
    wo_rm = remote(wout.at[0, :, others], wo.at[heads:], wo_s.at[0], wo_r.at[0], mate)
    res_rm = remote(acts.at[0, :, others], res.at[c], wo_s.at[1], wo_r.at[1], mate)
    res_in = remote(acts.at[0, :, mine], res.at[1 - c], wo_s.at[1], wo_r.at[1], mate)
    wo_rm.start()
    res_rm.start()

    kall[cached:, :] = jnp.zeros((4 * rows, HD), BF16)
    vall[cached:, :] = jnp.zeros((4 * rows, HD), BF16)
    for cp in small:
        cp.wait()
    lane = lax.broadcasted_iota(jnp.int32, (rows, HD), 1)
    sign = jnp.where(lane < HD // 2, -1.0, 1.0).astype(F32)
    row = lax.broadcasted_iota(jnp.int32, (rows, HD), 0)

    def tables(k, _):
        rel, b = lax.div(k, 2), lax.rem(k, 2)
        side = hi + rel - 2 * hi * rel
        pos = bidx[0] * (4 * rows) + (2 * side + b) * rows + row
        angle = pos.astype(F32) * freq[...]
        turns = jnp.floor(angle * np.float32(1.0 / (2.0 * math.pi)) + 0.5)
        angle = ((angle - turns * TURN[0]) - turns * TURN[1]) - turns * TURN[2]
        ct[span(k * rows, rows), :] = jnp.cos(angle)
        st[span(k * rows, rows), :] = jnp.sin(angle) * sign
        return 0

    lax.fori_loop(0, 4, tables, 0)
    none = F32(-jnp.inf)
    own_first = jnp.where(hi == 0, F32(0.0), none)
    other_first = jnp.where(hi == 1, F32(0.0), none)
    key_id = lax.broadcasted_iota(jnp.int32, bias.shape, 1)
    bias[...] = jnp.where(key_id < cached, jnp.where(key_id < vlen[0], F32(0.0), none), own_first)

    def project(x, rel, start, count, tiles=(2, 0, 1)):
        for n in tiles:
            y = jnp.dot(x, wq[:, 2 * n * HD : 2 * (n + 1) * HD], preferred_element_type=F32)
            for i in range(count):
                tok = span(2 * rel * rows + (start + i) * part, part)
                key_at = span(cached + 2 * rel * rows + (start + i) * part, part)
                cos, sin = ct[tok, :], st[tok, :]
                yb = y[i * part : (i + 1) * part]

                def turned(v):
                    return (v * cos + pltpu.roll(v, HD // 2, 1) * sin).astype(BF16)

                if n < 2:
                    for k in range(2):
                        at = (2 * n + k) * part
                        qb[rel, start + i, at : at + part, :] = turned(yb[:, k * HD : (k + 1) * HD])
                else:
                    kall[key_at, :] = turned(yb[:, :HD])
                    vall[key_at, :] = yb[:, HD:].astype(BF16)

    factor = np.float32(math.log2(math.e) / math.sqrt(HD))
    nt = (((1,), (1,)), ((), ()))
    near = cached + 2 * rows

    def att_copy(rel, r):
        k = 4 * rel + r
        at = span(r * part, part)
        return remote(att.at[rel, at, :heads], att.at[rel, at, heads:], at_s.at[k], at_r.at[k], mate)

    def hand_over(rel, r, o):
        at = span(r * part, part)
        for k in range(GROUP):
            att[rel, at, k * HD : (k + 1) * HD] = o[k * part : (k + 1) * part]
        att_copy(rel, r).start()

    def causal(r):
        qid = lax.rem(lax.broadcasted_iota(jnp.int32, (GROUP * part, 1), 0), part) + r * part
        return lax.broadcasted_iota(jnp.int32, (1, 2 * rows), 1) <= qid

    def softmax(sa, sb):
        m = jnp.maximum(jnp.max(sa, -1, keepdims=True), jnp.max(sb, -1, keepdims=True))
        ea = jnp.exp2((sa - m) * factor)
        eb = jnp.exp2((sb - m) * factor)
        return m, ea.astype(BF16), eb.astype(BF16), jnp.sum(ea, -1, keepdims=True) + jnp.sum(eb, -1, keepdims=True)

    def attend(r, _=0):
        q = qb[1, r]
        sa = lax.dot_general(q, kall[:near], nt, preferred_element_type=F32) + bias[...]
        sb = lax.dot_general(q, kall[near:], nt, preferred_element_type=F32)
        sb = jnp.where(causal(r), sb, none)
        _, ea, eb, tot = softmax(sa, sb)
        o = jnp.dot(ea, vall[:near], preferred_element_type=F32)
        o = o + jnp.dot(eb, vall[near:], preferred_element_type=F32)
        hand_over(1, r, (o / tot).astype(BF16))
        return 0

    def own_begin(r, _):
        q = qb[0, r]
        sa = lax.dot_general(q, kall[:cached], nt, preferred_element_type=F32) + bias[:, :cached]
        sb = lax.dot_general(q, kall[cached:near], nt, preferred_element_type=F32)
        sb = jnp.where(causal(r), sb, none)
        m, ea, eb, tot = softmax(sa, sb)
        o = jnp.dot(ea, vall[:cached], preferred_element_type=F32)
        acc[r] = o + jnp.dot(eb, vall[cached:near], preferred_element_type=F32)
        top[r] = m
        total[r] = tot
        return 0

    def own_more(r, core):
        keys = slice(near + core * rows, near + (core + 1) * rows)
        sa = lax.dot_general(qb[0, r], kall[keys], nt, preferred_element_type=F32) + other_first
        m = jnp.maximum(top[r], jnp.max(sa, -1, keepdims=True))
        scale = jnp.exp2((top[r] - m) * factor)
        ea = jnp.exp2((sa - m) * factor)
        o = acc[r] * scale + jnp.dot(ea.astype(BF16), vall[keys], preferred_element_type=F32)
        return m, total[r] * scale + jnp.sum(ea, -1, keepdims=True), o

    def own_middle(r, _):
        m, tot, o = own_more(r, 0)
        acc[r] = o
        top[r] = m
        total[r] = tot
        return 0

    def own_end(r):
        _, tot, o = own_more(r, 1)
        hand_over(0, r, (o / tot).astype(BF16))

    def piece(f):
        return span(f * PIECE, PIECE)

    def sum_copy(f):
        return remote(snd.at[piece(f)], rcv.at[piece(f)], rs_s.at[f], rs_r.at[f], sum_dev)

    def base_copy(f):
        return remote(bsnd.at[piece(f)], brcv.at[piece(f)], bs_s.at[f], bs_r.at[f], base_dev)

    def other_output(b):
        for i in range(2):
            att_copy(1, 2 * b + i).wait_recv()
        at = pl.ds(b * rows, rows)
        x = att[1, at, :]
        tile = wide // 8
        for n in range(8):
            cols = slice(n * tile, (n + 1) * tile)
            snd[at, cols] = jnp.dot(x, wo[:, cols], preferred_element_type=F32).astype(BF16)

    def send_sums(r):
        for i in range(per):
            sum_copy(r * per + i).start()

    def own_output(b):
        for i in range(2):
            att_copy(0, 2 * b + i).wait_recv()
        at = pl.ds(b * rows, rows)
        x = att[0, at, :]
        tile = wide // 8
        for n in range(8):
            cols = slice(n * tile, (n + 1) * tile)
            y = jnp.dot(x, wo[:, cols], preferred_element_type=F32)
            base[at, cols] = y + res[b, :, cols].astype(F32)

        @pl.when(special)
        def _():
            bsnd[at, :] = base[at, :].astype(BF16)
            for i in range(2 * per):
                base_copy(2 * b * per + i).start()

    in_block = 2 * per

    def x_copy(f):
        b, k = lax.div(f, in_block), lax.rem(f, in_block)
        return remote(
            fin.at[piece(f)], out.at[0, piece(k), mine], x_s.at[f], x_r.at[c * in_block + k], (nxt, 2 * hi + b)
        )

    def finish(f, _):
        sum_copy(f).wait_recv()

        @pl.when(special)
        def _():
            base_copy(f).wait_recv()
            fin[piece(f), :] = (brcv[piece(f), :].astype(F32) + rcv[piece(f), :].astype(F32)).astype(BF16)

        @pl.when(jnp.logical_not(special))
        def _():
            fin[piece(f), :] = (base[piece(f), :] + rcv[piece(f), :].astype(F32)).astype(BF16)

        x_copy(f).start()
        return 0

    def other_rows(j):
        return nrm[2 + lax.div(j, 2), span(lax.rem(j, 2) * part, part), :]

    mate_arrival(1 - c).wait_recv()
    mate_arrival(3 - c).wait_recv()
    wq_cp.wait()
    project(nrm[0:2].reshape(2 * rows, dim), 0, 0, 4)
    k_cp.wait()
    v_cp.wait()
    lax.fori_loop(0, 4, own_begin, 0)
    wo_cp.wait()
    wo_rm.wait_recv()
    res_cp.wait()
    res_in.wait_recv()

    for j in range(2):
        arrived(j).wait_recv()
        passed_on(j, c).start()

    @pl.when(relays)
    def _():
        relay_out(0).wait_recv()
        relay_in().start()

    for j in range(2):
        passed_on(j, 1 - c).wait_recv()
    project(nrm[2], 1, 0, 2)
    lax.fori_loop(0, 2, attend, 0)
    lax.fori_loop(0, 4, own_middle, 0)
    other_output(0)

    @pl.when(jnp.logical_not(special))
    def _():
        send_sums(0)
        send_sums(1)

    arrived(2).wait_recv()
    passed_on(2, c).start()
    passed_on(2, 1 - c).wait_recv()
    project(other_rows(2), 1, 2, 1)
    attend(2)

    @pl.when(special)
    def _():
        for q in range(len(HELPERS)):
            relay_arrival(q).wait_recv()

        def held(r, _):
            send_sums(r)
            return 0

        lax.fori_loop(0, 2, held, 0)

    @pl.when(jnp.logical_not(special))
    def _():
        arrived(3).wait_recv()

    passed_on(3, c).start()
    passed_on(3, 1 - c).wait_recv()
    project(other_rows(3), 1, 3, 1, (2,))
    own_end(0)
    own_end(1)
    project(other_rows(3), 1, 3, 1, (0, 1))
    own_output(0)
    finish(0, 0)
    finish(1, 0)
    own_end(2)
    own_end(3)
    attend(3)
    finish(2, 0)
    own_output(1)
    finish(3, 0)
    other_output(1)
    send_sums(2)
    send_sums(3)
    lax.fori_loop(4, pieces, finish, 0)

    for j in range(AG):
        if j < 3:
            ag_copy(j).wait_send()
        mate_copy(j).wait_send()
        passed_on(j, c).wait_send()

    @pl.when(special)
    def _():
        for q in range(len(HELPERS)):
            relay_out(q).wait_send()

    @pl.when(jnp.logical_not(special))
    def _():
        ag_copy(3).wait_send()

    @pl.when(relays)
    def _():
        relay_in().wait_send()

    wo_rm.wait_send()
    res_rm.wait_send()
    for rel in range(2):
        for r in range(4):
            att_copy(rel, r).wait_send()

    def drain(f, _):
        sum_copy(f).wait_send()
        x_copy(f).wait_send()
        return 0

    lax.fori_loop(0, pieces, drain, 0)

    @pl.when(special)
    def _():
        def drain_base(f, _):
            base_copy(f).wait_send()
            return 0

        lax.fori_loop(0, pieces, drain_base, 0)

    def arrive(k, _):
        side, f = lax.div(k, in_block), lax.rem(k, in_block)
        cols = span(side * wide, wide)
        remote(fin.at[piece(f)], out.at[0, piece(f), cols], x_s.at[k], x_r.at[k], mate).wait_recv()
        return 0

    lax.fori_loop(0, 2 * in_block, arrive, 0)


def split_turn():
    whole, parts = 2.0 * math.pi, []
    for _ in range(2):
        scale = 2.0 ** (math.frexp(whole)[1] - 10)
        part = math.floor(whole / scale) * scale
        parts.append(np.float32(part))
        whole -= part
    return (*parts, np.float32(whole))


TURN = split_turn()


def body(sections, acts, norm_gain, w_qkv, w_out, kv_cache, block_index, valid_len):
    rows, dim = acts.shape[1:]
    wide = dim // 2
    cached = kv_cache.shape[1]
    width = w_qkv.shape[2]
    heads = w_out.shape[1]
    exponent = 2.0 * (np.arange(HD) % (HD // 2)) / HD
    freq = jnp.asarray(np.exp(-np.log(500000.0) * exponent).astype(np.float32)[None])
    step = rows // 2
    pieces = 2 * rows // PIECE
    keys = cached + 4 * rows
    dma = pltpu.SemaphoreType.DMA
    hbm = pl.BlockSpec(memory_space=pltpu.HBM)
    return pl.pallas_call(
        functools.partial(kernel, sections),
        out_shape=pltpu.VMEM((1, rows, dim), BF16),
        in_specs=[hbm] * 8,
        out_specs=pl.BlockSpec(memory_space=pltpu.VMEM),
        scratch_shapes=[
            pltpu.SMEM((1,), jnp.int32),
            pltpu.SMEM((1,), jnp.int32),
            pltpu.VMEM((1, HD), F32),
            pltpu.VMEM((rows, dim), BF16),
            pltpu.VMEM((1, dim), F32),
            pltpu.VMEM((4, rows, dim), BF16),
            pltpu.VMEM((dim, width), BF16),
            pltpu.VMEM((2 * heads, wide), BF16),
            pltpu.VMEM((keys, HD), BF16),
            pltpu.VMEM((keys, HD), BF16),
            pltpu.VMEM((1, cached + 2 * rows), F32),
            pltpu.VMEM((4 * rows, HD), F32),
            pltpu.VMEM((4 * rows, HD), F32),
            pltpu.VMEM((2, 4, GROUP * step, HD), BF16),
            pltpu.VMEM((4, GROUP * step, HD), F32),
            pltpu.VMEM((4, GROUP * step, 1), F32),
            pltpu.VMEM((4, GROUP * step, 1), F32),
            pltpu.VMEM((2, 2 * rows, 2 * heads), BF16),
            pltpu.VMEM((2, rows, wide), BF16),
            pltpu.VMEM((2 * rows, wide), F32),
            pltpu.VMEM((2 * rows, wide), BF16),
            pltpu.VMEM((2 * rows, wide), BF16),
            pltpu.VMEM((2 * rows, wide), BF16),
            pltpu.VMEM((2 * rows, wide), BF16),
            pltpu.VMEM((2 * rows, wide), BF16),
            pltpu.VMEM((rows // AG, dim // len(HELPERS)), BF16),
            dma((AG + 9,)),
            dma((AG,)), dma((AG,)), dma((AG,)), dma((AG,)), dma((AG,)), dma((AG,)),
            dma((2,)), dma((2,)), dma((8,)), dma((8,)),
            dma((pieces,)), dma((pieces,)), dma((pieces,)), dma((pieces,)), dma((pieces,)), dma((pieces,)),
            dma((len(HELPERS),)), dma((1,)), dma((1,)), dma((len(HELPERS),)),
        ],
        compiler_params=pltpu.CompilerParams(
            collective_id=0, has_side_effects=True, vmem_limit_bytes=56 * 2**20
        ),
    )(block_index, valid_len, freq, acts, norm_gain, w_qkv, w_out, kv_cache)

def solution(mesh):
    in_specs = (
        P("section", "tensor", None),
        P("section", None),
        P("section", None, "tensor"),
        P("section", "tensor", None),
        P("section", None, "tensor"),
        P("section"),
        P("section"),
    )
    out_specs = P("section", "tensor", None)
    return jax.shard_map(
        functools.partial(body, mesh.shape["section"]),
        mesh=mesh, in_specs=in_specs, out_specs=out_specs, check_vma=False,
    )
```

```python
import functools
import math

import jax
import jax.numpy as jnp
import numpy as np
from jax import lax
from jax.experimental import pallas as pl
from jax.experimental.pallas import tpu as pltpu
from jax.sharding import PartitionSpec as P

HELPERS = (30, 27, 26, 23)
GROUP = 4
HD = 128
AG = 4
PIECE = 16
MESH = pl.DeviceIdType.MESH
F32 = jnp.float32
BF16 = jnp.bfloat16


def kernel(
    sections, bidx_in, vlen_in, freq_in, acts, gain, wqkv, wout, cache, out,
    bidx, vlen, freq, a_v, g_v, nrm, wq, wo, kall, vall, bias, ct, st, qb, acc, top, total, att, res, base, snd, rcv, bsnd, brcv, fin, relay,
    l_sem, ag_s, ag_r, mt_s, mt_r, fw_s, fw_r, wo_s, wo_r, at_s, at_r, rs_s, rs_r, bs_s, bs_r, x_s, x_r, ro_s, ro_r, ri_s, ri_r,
):
    rows, dim = a_v.shape
    wide = dim // 2
    chunk = rows // AG
    part = rows // 2
    per = part // PIECE
    half = sections // 2
    cached = cache.shape[1]
    heads = wout.shape[1]
    pieces = 4 * per

    s = lax.axis_index("section")
    t = lax.axis_index("tensor")
    c = lax.rem(t, 2)
    hi = lax.div(t, 2)
    low = lax.rem(s, half)
    last = lax.div(low, half - 1)
    nxt = s - low + lax.rem(low + 1, half)
    prv = s - low + lax.rem(low + half - 1, half)
    oth = lax.rem(s + half, sections)
    mate = (s, 2 * hi + 1 - c)
    partner = (s, 2 * (1 - hi) + c)
    sum_dev = (lax.rem(s + half * last, sections), 2 * (1 - hi) + c)
    base_dev = (oth, t)
    first = s - low
    ends = first + half - 1
    helper = [low == k for k in HELPERS]
    relays = functools.reduce(jnp.logical_or, helper)
    quarter = sum(jnp.where(helper[q], q, 0) for q in range(1, len(HELPERS)))
    cross_dev = (oth, 2 * (1 - hi) + c)
    special = last == 1

    def remote(src, dst, ss, rs, dev):
        return pltpu.make_async_remote_copy(
            src_ref=src, dst_ref=dst, send_sem=ss, recv_sem=rs, device_id=dev, device_id_type=MESH
        )

    def span(start, size):
        return pl.ds(pl.multiple_of(start, size), size)

    mine = span(c * wide, wide)
    others = span((1 - c) * wide, wide)
    g_cp = pltpu.make_async_copy(gain, g_v, l_sem.at[AG])
    a_cp = [
        pltpu.make_async_copy(
            acts.at[0, pl.ds(j * chunk, chunk)], a_v.at[pl.ds(j * chunk, chunk)], l_sem.at[j]
        )
        for j in range(AG)
    ]
    a_cp[0].start()
    g_cp.start()
    small = [
        pltpu.make_async_copy(src, dst, l_sem.at[AG + 6 + i])
        for i, (src, dst) in enumerate(((bidx_in, bidx), (vlen_in, vlen), (freq_in, freq)))
    ]
    for j in range(1, AG):
        a_cp[j].start()

    barrier = pltpu.get_barrier_semaphore()
    for dev in (partner, mate, (prv, 2 * hi), (prv, 2 * hi + 1)):
        pl.semaphore_signal(barrier, inc=1, device_id=dev, device_id_type=MESH)

    @pl.when(special)
    def _():
        for dev in (base_dev, cross_dev, *[(first + k, t) for k in HELPERS]):
            pl.semaphore_signal(barrier, inc=1, device_id=dev, device_id_type=MESH)

    @pl.when(relays)
    def _():
        pl.semaphore_signal(barrier, inc=1, device_id=(ends, 2 * (1 - hi) + c), device_id_type=MESH)

    wq_cp = pltpu.make_async_copy(wqkv.at[0], wq, l_sem.at[AG + 1])
    k_cp = pltpu.make_async_copy(cache.at[0, :, :HD], kall.at[:cached], l_sem.at[AG + 2])
    v_cp = pltpu.make_async_copy(cache.at[0, :, HD:], vall.at[:cached], l_sem.at[AG + 3])
    wo_cp = pltpu.make_async_copy(wout.at[0, :, mine], wo.at[:heads], l_sem.at[AG + 4])
    res_cp = pltpu.make_async_copy(acts.at[0, :, mine], res.at[c], l_sem.at[AG + 5])
    wq_cp.start()
    k_cp.start()
    v_cp.start()
    for cp in small:
        cp.start()

    def ag_copy(j):
        r = span((2 * (j % 2) + c) * chunk, chunk)
        return remote(nrm.at[j // 2, r], nrm.at[2 + j // 2, r], ag_s.at[j], ag_r.at[j], partner)

    def mate_copy(k):
        r = span(k * chunk, chunk)
        return remote(nrm.at[c, r], nrm.at[c, r], mt_s.at[k], mt_r.at[k], mate)

    def mate_arrival(k):
        r = span(k * chunk, chunk)
        return remote(nrm.at[1 - c, r], nrm.at[1 - c, r], mt_s.at[k], mt_r.at[k], mate)

    def passed_on(j, core):
        slot, r = 2 + lax.div(j, 2), span((2 * lax.rem(j, 2) + core) * chunk, chunk)
        return remote(nrm.at[slot, r], nrm.at[slot, r], fw_s.at[j], fw_r.at[j], mate)

    def arrived(j):
        slot, r = 2 + lax.div(j, 2), span((2 * lax.rem(j, 2) + c) * chunk, chunk)
        return remote(nrm.at[slot, r], nrm.at[slot, r], ag_s.at[j], ag_r.at[j], partner)

    qw = dim // len(HELPERS)
    late = span((2 + c) * chunk, chunk)

    def relay_out(q):
        return remote(
            nrm.at[1, late, pl.ds(q * qw, qw)], relay, ro_s.at[q], ro_r.at[0],
            (first + HELPERS[q], 2 * (1 - hi) + c),
        )

    def relay_in():
        return remote(relay, nrm.at[3, late, span(quarter * qw, qw)], ri_s.at[0], ri_r.at[quarter], (ends, t))

    def relay_arrival(q):
        return remote(relay, nrm.at[3, late, pl.ds(q * qw, qw)], ri_s.at[0], ri_r.at[q], mate)

    g_cp.wait()
    for j in range(AG):
        a_cp[j].wait()
        r = pl.ds(j * chunk, chunk)
        x = a_v[r, :].astype(F32)
        ms = jnp.mean(x * x, -1, keepdims=True)
        nrm[c, r, :] = (x * lax.rsqrt(ms + 1e-05) * g_v[...]).astype(BF16)

    pl.semaphore_wait(barrier, 4 + (2 + len(HELPERS)) * last + jnp.where(relays, 1, 0))

    @pl.when(c == 0)
    def _():
        ag_copy(0).start()
        ag_copy(1).start()

    mate_copy(1 - c).start()
    mate_copy(3 - c).start()
    mate_arrival(c).wait_recv()
    mate_arrival(c + 2).wait_recv()

    @pl.when(c == 1)
    def _():
        ag_copy(0).start()
        ag_copy(1).start()

    ag_copy(2).start()

    @pl.when(special)
    def _():
        for q in range(len(HELPERS)):
            relay_out(q).start()

    @pl.when(jnp.logical_not(special))
    def _():
        ag_copy(3).start()

    mate_copy(c).start()
    mate_copy(c + 2).start()

    wo_cp.start()
    res_cp.start()
    wo_rm = remote(wout.at[0, :, others], wo.at[heads:], wo_s.at[0], wo_r.at[0], mate)
    res_rm = remote(acts.at[0, :, others], res.at[c], wo_s.at[1], wo_r.at[1], mate)
    res_in = remote(acts.at[0, :, mine], res.at[1 - c], wo_s.at[1], wo_r.at[1], mate)
    wo_rm.start()
    res_rm.start()

    kall[cached:, :] = jnp.zeros((4 * rows, HD), BF16)
    vall[cached:, :] = jnp.zeros((4 * rows, HD), BF16)
    for cp in small:
        cp.wait()
    lane = lax.broadcasted_iota(jnp.int32, (rows, HD), 1)
    sign = jnp.where(lane < HD // 2, -1.0, 1.0).astype(F32)
    row = lax.broadcasted_iota(jnp.int32, (rows, HD), 0)

    def tables(k, _):
        rel, b = lax.div(k, 2), lax.rem(k, 2)
        side = hi + rel - 2 * hi * rel
        pos = bidx[0] * (4 * rows) + (2 * side + b) * rows + row
        angle = pos.astype(F32) * freq[...]
        turns = jnp.floor(angle * np.float32(1.0 / (2.0 * math.pi)) + 0.5)
        angle = ((angle - turns * TURN[0]) - turns * TURN[1]) - turns * TURN[2]
        ct[span(k * rows, rows), :] = jnp.cos(angle)
        st[span(k * rows, rows), :] = jnp.sin(angle) * sign
        return 0

    lax.fori_loop(0, 4, tables, 0)
    none = F32(-jnp.inf)
    own_first = jnp.where(hi == 0, F32(0.0), none)
    other_first = jnp.where(hi == 1, F32(0.0), none)
    key_id = lax.broadcasted_iota(jnp.int32, bias.shape, 1)
    bias[...] = jnp.where(key_id < cached, jnp.where(key_id < vlen[0], F32(0.0), none), own_first)

    def project(x, rel, start, count, tiles=(2, 0, 1)):
        for n in tiles:
            y = jnp.dot(x, wq[:, 2 * n * HD : 2 * (n + 1) * HD], preferred_element_type=F32)
            for i in range(count):
                tok = span(2 * rel * rows + (start + i) * part, part)
                key_at = span(cached + 2 * rel * rows + (start + i) * part, part)
                cos, sin = ct[tok, :], st[tok, :]
                yb = y[i * part : (i + 1) * part]

                def turned(v):
                    return (v * cos + pltpu.roll(v, HD // 2, 1) * sin).astype(BF16)

                if n < 2:
                    for k in range(2):
                        at = (2 * n + k) * part
                        qb[rel, start + i, at : at + part, :] = turned(yb[:, k * HD : (k + 1) * HD])
                else:
                    kall[key_at, :] = turned(yb[:, :HD])
                    vall[key_at, :] = yb[:, HD:].astype(BF16)

    factor = np.float32(math.log2(math.e) / math.sqrt(HD))
    nt = (((1,), (1,)), ((), ()))
    near = cached + 2 * rows

    def att_copy(rel, r):
        k = 4 * rel + r
        at = span(r * part, part)
        return remote(att.at[rel, at, :heads], att.at[rel, at, heads:], at_s.at[k], at_r.at[k], mate)

    def hand_over(rel, r, o):
        at = span(r * part, part)
        for k in range(GROUP):
            att[rel, at, k * HD : (k + 1) * HD] = o[k * part : (k + 1) * part]
        att_copy(rel, r).start()

    def causal(r):
        qid = lax.rem(lax.broadcasted_iota(jnp.int32, (GROUP * part, 1), 0), part) + r * part
        return lax.broadcasted_iota(jnp.int32, (1, 2 * rows), 1) <= qid

    def softmax(sa, sb):
        m = jnp.maximum(jnp.max(sa, -1, keepdims=True), jnp.max(sb, -1, keepdims=True))
        ea = jnp.exp2((sa - m) * factor)
        eb = jnp.exp2((sb - m) * factor)
        return m, ea.astype(BF16), eb.astype(BF16), jnp.sum(ea, -1, keepdims=True) + jnp.sum(eb, -1, keepdims=True)

    def attend(r, _=0):
        q = qb[1, r]
        sa = lax.dot_general(q, kall[:near], nt, preferred_element_type=F32) + bias[...]
        sb = lax.dot_general(q, kall[near:], nt, preferred_element_type=F32)
        sb = jnp.where(causal(r), sb, none)
        _, ea, eb, tot = softmax(sa, sb)
        o = jnp.dot(ea, vall[:near], preferred_element_type=F32)
        o = o + jnp.dot(eb, vall[near:], preferred_element_type=F32)
        hand_over(1, r, (o / tot).astype(BF16))
        return 0

    def own_begin(r, _):
        q = qb[0, r]
        sa = lax.dot_general(q, kall[:cached], nt, preferred_element_type=F32) + bias[:, :cached]
        sb = lax.dot_general(q, kall[cached:near], nt, preferred_element_type=F32)
        sb = jnp.where(causal(r), sb, none)
        m, ea, eb, tot = softmax(sa, sb)
        o = jnp.dot(ea, vall[:cached], preferred_element_type=F32)
        acc[r] = o + jnp.dot(eb, vall[cached:near], preferred_element_type=F32)
        top[r] = m
        total[r] = tot
        return 0

    def own_more(r, core):
        keys = slice(near + core * rows, near + (core + 1) * rows)
        sa = lax.dot_general(qb[0, r], kall[keys], nt, preferred_element_type=F32) + other_first
        m = jnp.maximum(top[r], jnp.max(sa, -1, keepdims=True))
        scale = jnp.exp2((top[r] - m) * factor)
        ea = jnp.exp2((sa - m) * factor)
        o = acc[r] * scale + jnp.dot(ea.astype(BF16), vall[keys], preferred_element_type=F32)
        return m, total[r] * scale + jnp.sum(ea, -1, keepdims=True), o

    def own_middle(r, _):
        m, tot, o = own_more(r, 0)
        acc[r] = o
        top[r] = m
        total[r] = tot
        return 0

    def own_end(r):
        _, tot, o = own_more(r, 1)
        hand_over(0, r, (o / tot).astype(BF16))

    def piece(f):
        return span(f * PIECE, PIECE)

    def sum_copy(f):
        return remote(snd.at[piece(f)], rcv.at[piece(f)], rs_s.at[f], rs_r.at[f], sum_dev)

    def base_copy(f):
        return remote(bsnd.at[piece(f)], brcv.at[piece(f)], bs_s.at[f], bs_r.at[f], base_dev)

    def other_output(b):
        for i in range(2):
            att_copy(1, 2 * b + i).wait_recv()
        at = pl.ds(b * rows, rows)
        x = att[1, at, :]
        tile = wide // 8
        for n in range(8):
            cols = slice(n * tile, (n + 1) * tile)
            snd[at, cols] = jnp.dot(x, wo[:, cols], preferred_element_type=F32).astype(BF16)

    def send_sums(r):
        for i in range(per):
            sum_copy(r * per + i).start()

    def own_output(b):
        for i in range(2):
            att_copy(0, 2 * b + i).wait_recv()
        at = pl.ds(b * rows, rows)
        x = att[0, at, :]
        tile = wide // 8
        for n in range(8):
            cols = slice(n * tile, (n + 1) * tile)
            y = jnp.dot(x, wo[:, cols], preferred_element_type=F32)
            base[at, cols] = y + res[b, :, cols].astype(F32)

        @pl.when(special)
        def _():
            bsnd[at, :] = base[at, :].astype(BF16)
            for i in range(2 * per):
                base_copy(2 * b * per + i).start()

    in_block = 2 * per

    def x_copy(f):
        b, k = lax.div(f, in_block), lax.rem(f, in_block)
        return remote(
            fin.at[piece(f)], out.at[0, piece(k), mine], x_s.at[f], x_r.at[c * in_block + k], (nxt, 2 * hi + b)
        )

    def finish(f, _):
        sum_copy(f).wait_recv()

        @pl.when(special)
        def _():
            base_copy(f).wait_recv()
            fin[piece(f), :] = (brcv[piece(f), :].astype(F32) + rcv[piece(f), :].astype(F32)).astype(BF16)

        @pl.when(jnp.logical_not(special))
        def _():
            fin[piece(f), :] = (base[piece(f), :] + rcv[piece(f), :].astype(F32)).astype(BF16)

        x_copy(f).start()
        return 0

    mate_arrival(1 - c).wait_recv()
    mate_arrival(3 - c).wait_recv()
    wq_cp.wait()
    project(nrm[0:2].reshape(2 * rows, dim), 0, 0, 4)
    k_cp.wait()
    v_cp.wait()
    lax.fori_loop(0, 4, own_begin, 0)
    wo_cp.wait()
    wo_rm.wait_recv()
    res_cp.wait()
    res_in.wait_recv()

    for j in range(2):
        arrived(j).wait_recv()
        passed_on(j, c).start()

    @pl.when(relays)
    def _():
        relay_out(0).wait_recv()
        relay_in().start()

    for j in range(2):
        passed_on(j, 1 - c).wait_recv()
    project(nrm[2], 1, 0, 2)
    lax.fori_loop(0, 2, attend, 0)
    lax.fori_loop(0, 4, own_middle, 0)
    other_output(0)
    send_sums(0)
    send_sums(1)

    arrived(2).wait_recv()
    passed_on(2, c).start()

    @pl.when(special)
    def _():
        for q in range(len(HELPERS)):
            relay_arrival(q).wait_recv()

    @pl.when(jnp.logical_not(special))
    def _():
        arrived(3).wait_recv()

    passed_on(3, c).start()
    passed_on(2, 1 - c).wait_recv()
    passed_on(3, 1 - c).wait_recv()
    project(nrm[3], 1, 2, 2, (2,))
    own_end(0)
    own_end(1)
    project(nrm[3], 1, 2, 2, (0, 1))
    own_output(0)
    finish(0, 0)
    finish(1, 0)
    own_end(2)
    own_end(3)
    attend(2)
    finish(2, 0)
    own_output(1)
    attend(3)
    finish(3, 0)
    other_output(1)
    send_sums(2)
    send_sums(3)
    lax.fori_loop(4, pieces, finish, 0)

    for j in range(AG):
        if j < 3:
            ag_copy(j).wait_send()
        mate_copy(j).wait_send()
        passed_on(j, c).wait_send()

    @pl.when(special)
    def _():
        for q in range(len(HELPERS)):
            relay_out(q).wait_send()

    @pl.when(jnp.logical_not(special))
    def _():
        ag_copy(3).wait_send()

    @pl.when(relays)
    def _():
        relay_in().wait_send()

    wo_rm.wait_send()
    res_rm.wait_send()
    for rel in range(2):
        for r in range(4):
            att_copy(rel, r).wait_send()

    def drain(f, _):
        sum_copy(f).wait_send()
        x_copy(f).wait_send()
        return 0

    lax.fori_loop(0, pieces, drain, 0)

    @pl.when(special)
    def _():
        def drain_base(f, _):
            base_copy(f).wait_send()
            return 0

        lax.fori_loop(0, pieces, drain_base, 0)

    def arrive(k, _):
        side, f = lax.div(k, in_block), lax.rem(k, in_block)
        cols = span(side * wide, wide)
        remote(fin.at[piece(f)], out.at[0, piece(f), cols], x_s.at[k], x_r.at[k], mate).wait_recv()
        return 0

    lax.fori_loop(0, 2 * in_block, arrive, 0)


def split_turn():
    whole, parts = 2.0 * math.pi, []
    for _ in range(2):
        scale = 2.0 ** (math.frexp(whole)[1] - 10)
        part = math.floor(whole / scale) * scale
        parts.append(np.float32(part))
        whole -= part
    return (*parts, np.float32(whole))


TURN = split_turn()


def body(sections, acts, norm_gain, w_qkv, w_out, kv_cache, block_index, valid_len):
    rows, dim = acts.shape[1:]
    wide = dim // 2
    cached = kv_cache.shape[1]
    width = w_qkv.shape[2]
    heads = w_out.shape[1]
    exponent = 2.0 * (np.arange(HD) % (HD // 2)) / HD
    freq = jnp.asarray(np.exp(-np.log(500000.0) * exponent).astype(np.float32)[None])
    step = rows // 2
    pieces = 2 * rows // PIECE
    keys = cached + 4 * rows
    dma = pltpu.SemaphoreType.DMA
    hbm = pl.BlockSpec(memory_space=pltpu.HBM)
    return pl.pallas_call(
        functools.partial(kernel, sections),
        out_shape=pltpu.VMEM((1, rows, dim), BF16),
        in_specs=[hbm] * 8,
        out_specs=pl.BlockSpec(memory_space=pltpu.VMEM),
        scratch_shapes=[
            pltpu.SMEM((1,), jnp.int32),
            pltpu.SMEM((1,), jnp.int32),
            pltpu.VMEM((1, HD), F32),
            pltpu.VMEM((rows, dim), BF16),
            pltpu.VMEM((1, dim), F32),
            pltpu.VMEM((4, rows, dim), BF16),
            pltpu.VMEM((dim, width), BF16),
            pltpu.VMEM((2 * heads, wide), BF16),
            pltpu.VMEM((keys, HD), BF16),
            pltpu.VMEM((keys, HD), BF16),
            pltpu.VMEM((1, cached + 2 * rows), F32),
            pltpu.VMEM((4 * rows, HD), F32),
            pltpu.VMEM((4 * rows, HD), F32),
            pltpu.VMEM((2, 4, GROUP * step, HD), BF16),
            pltpu.VMEM((4, GROUP * step, HD), F32),
            pltpu.VMEM((4, GROUP * step, 1), F32),
            pltpu.VMEM((4, GROUP * step, 1), F32),
            pltpu.VMEM((2, 2 * rows, 2 * heads), BF16),
            pltpu.VMEM((2, rows, wide), BF16),
            pltpu.VMEM((2 * rows, wide), F32),
            pltpu.VMEM((2 * rows, wide), BF16),
            pltpu.VMEM((2 * rows, wide), BF16),
            pltpu.VMEM((2 * rows, wide), BF16),
            pltpu.VMEM((2 * rows, wide), BF16),
            pltpu.VMEM((2 * rows, wide), BF16),
            pltpu.VMEM((rows // AG, dim // len(HELPERS)), BF16),
            dma((AG + 9,)),
            dma((AG,)), dma((AG,)), dma((AG,)), dma((AG,)), dma((AG,)), dma((AG,)),
            dma((2,)), dma((2,)), dma((8,)), dma((8,)),
            dma((pieces,)), dma((pieces,)), dma((pieces,)), dma((pieces,)), dma((pieces,)), dma((pieces,)),
            dma((len(HELPERS),)), dma((1,)), dma((1,)), dma((len(HELPERS),)),
        ],
        compiler_params=pltpu.CompilerParams(
            collective_id=0, has_side_effects=True, vmem_limit_bytes=56 * 2**20
        ),
    )(block_index, valid_len, freq, acts, norm_gain, w_qkv, w_out, kv_cache)

def solution(mesh):
    in_specs = (
        P("section", "tensor", None),
        P("section", None),
        P("section", None, "tensor"),
        P("section", "tensor", None),
        P("section", None, "tensor"),
        P("section"),
        P("section"),
    )
    out_specs = P("section", "tensor", None)
    return jax.shard_map(
        functools.partial(body, mesh.shape["section"]),
        mesh=mesh, in_specs=in_specs, out_specs=out_specs, check_vma=False,
    )
```

```python
import functools
import math

import jax
import jax.numpy as jnp
import numpy as np
from jax import lax
from jax.experimental import pallas as pl
from jax.experimental.pallas import tpu as pltpu
from jax.sharding import PartitionSpec as P

HELPERS = (30, 27, 26, 23)
GROUP = 4
HD = 128
AG = 4
PIECE = 16
MESH = pl.DeviceIdType.MESH
F32 = jnp.float32
BF16 = jnp.bfloat16


def kernel(
    sections, bidx_in, vlen_in, freq_in, acts, gain, wqkv, wout, cache, out,
    bidx, vlen, freq, a_v, g_v, nrm, wq, wo, kall, vall, bias, ct, st, qb, acc, top, total, att, res, base, snd, rcv, bsnd, brcv, fin, relay,
    l_sem, ag_s, ag_r, mt_s, mt_r, fw_s, fw_r, wo_s, wo_r, at_s, at_r, rs_s, rs_r, bs_s, bs_r, x_s, x_r, ro_s, ro_r, ri_s, ri_r,
):
    rows, dim = a_v.shape
    wide = dim // 2
    chunk = rows // AG
    part = rows // 2
    per = part // PIECE
    half = sections // 2
    cached = cache.shape[1]
    heads = wout.shape[1]
    pieces = 4 * per

    s = lax.axis_index("section")
    t = lax.axis_index("tensor")
    c = lax.rem(t, 2)
    hi = lax.div(t, 2)
    low = lax.rem(s, half)
    last = lax.div(low, half - 1)
    nxt = s - low + lax.rem(low + 1, half)
    prv = s - low + lax.rem(low + half - 1, half)
    oth = lax.rem(s + half, sections)
    mate = (s, 2 * hi + 1 - c)
    partner = (s, 2 * (1 - hi) + c)
    sum_dev = (lax.rem(s + half * last, sections), 2 * (1 - hi) + c)
    base_dev = (oth, t)
    first = s - low
    ends = first + half - 1
    helper = [low == k for k in HELPERS]
    relays = functools.reduce(jnp.logical_or, helper)
    quarter = sum(jnp.where(helper[q], q, 0) for q in range(1, len(HELPERS)))
    cross_dev = (oth, 2 * (1 - hi) + c)
    special = last == 1

    def remote(src, dst, ss, rs, dev):
        return pltpu.make_async_remote_copy(
            src_ref=src, dst_ref=dst, send_sem=ss, recv_sem=rs, device_id=dev, device_id_type=MESH
        )

    def span(start, size):
        return pl.ds(pl.multiple_of(start, size), size)

    mine = span(c * wide, wide)
    others = span((1 - c) * wide, wide)
    g_cp = pltpu.make_async_copy(gain, g_v, l_sem.at[AG])
    a_cp = [
        pltpu.make_async_copy(
            acts.at[0, pl.ds(j * chunk, chunk)], a_v.at[pl.ds(j * chunk, chunk)], l_sem.at[j]
        )
        for j in range(AG)
    ]
    a_cp[0].start()
    g_cp.start()
    small = [
        pltpu.make_async_copy(src, dst, l_sem.at[AG + 6 + i])
        for i, (src, dst) in enumerate(((bidx_in, bidx), (vlen_in, vlen), (freq_in, freq)))
    ]
    for j in range(1, AG):
        a_cp[j].start()

    barrier = pltpu.get_barrier_semaphore()
    for dev in (partner, mate, (prv, 2 * hi), (prv, 2 * hi + 1)):
        pl.semaphore_signal(barrier, inc=1, device_id=dev, device_id_type=MESH)

    @pl.when(special)
    def _():
        for dev in (base_dev, cross_dev, *[(first + k, t) for k in HELPERS]):
            pl.semaphore_signal(barrier, inc=1, device_id=dev, device_id_type=MESH)

    @pl.when(relays)
    def _():
        pl.semaphore_signal(barrier, inc=1, device_id=(ends, 2 * (1 - hi) + c), device_id_type=MESH)

    wq_cp = pltpu.make_async_copy(wqkv.at[0], wq, l_sem.at[AG + 1])
    k_cp = pltpu.make_async_copy(cache.at[0, :, :HD], kall.at[:cached], l_sem.at[AG + 2])
    v_cp = pltpu.make_async_copy(cache.at[0, :, HD:], vall.at[:cached], l_sem.at[AG + 3])
    wo_cp = pltpu.make_async_copy(wout.at[0, :, mine], wo.at[:heads], l_sem.at[AG + 4])
    res_cp = pltpu.make_async_copy(acts.at[0, :, mine], res.at[c], l_sem.at[AG + 5])
    wq_cp.start()
    k_cp.start()
    v_cp.start()
    for cp in small:
        cp.start()

    def ag_copy(j):
        r = span((2 * (j % 2) + c) * chunk, chunk)
        return remote(nrm.at[j // 2, r], nrm.at[2 + j // 2, r], ag_s.at[j], ag_r.at[j], partner)

    def mate_copy(k):
        r = span(k * chunk, chunk)
        return remote(nrm.at[c, r], nrm.at[c, r], mt_s.at[k], mt_r.at[k], mate)

    def mate_arrival(k):
        r = span(k * chunk, chunk)
        return remote(nrm.at[1 - c, r], nrm.at[1 - c, r], mt_s.at[k], mt_r.at[k], mate)

    def passed_on(j, core):
        slot, r = 2 + lax.div(j, 2), span((2 * lax.rem(j, 2) + core) * chunk, chunk)
        return remote(nrm.at[slot, r], nrm.at[slot, r], fw_s.at[j], fw_r.at[j], mate)

    def arrived(j):
        slot, r = 2 + lax.div(j, 2), span((2 * lax.rem(j, 2) + c) * chunk, chunk)
        return remote(nrm.at[slot, r], nrm.at[slot, r], ag_s.at[j], ag_r.at[j], partner)

    qw = dim // len(HELPERS)
    ways = len(HELPERS)

    def late(i):
        return span((2 * i + c) * chunk, chunk)

    def relay_out(q, i):
        return remote(
            nrm.at[1, late(i), pl.ds(q * qw, qw)], relay.at[i], ro_s.at[i * ways + q], ro_r.at[i],
            (first + HELPERS[q], 2 * (1 - hi) + c),
        )

    def relay_in(i):
        return remote(
            relay.at[i], nrm.at[3, late(i), span(quarter * qw, qw)], ri_s.at[i], ri_r.at[i * ways + quarter], (ends, t)
        )

    def relay_arrival(q, i):
        return remote(
            relay.at[i], nrm.at[3, late(i), pl.ds(q * qw, qw)], ri_s.at[i], ri_r.at[i * ways + q], mate
        )

    g_cp.wait()
    for j in range(AG):
        a_cp[j].wait()
        r = pl.ds(j * chunk, chunk)
        x = a_v[r, :].astype(F32)
        ms = jnp.mean(x * x, -1, keepdims=True)
        nrm[c, r, :] = (x * lax.rsqrt(ms + 1e-05) * g_v[...]).astype(BF16)

    pl.semaphore_wait(barrier, 4 + (2 + len(HELPERS)) * last + jnp.where(relays, 1, 0))

    @pl.when(c == 0)
    def _():
        ag_copy(0).start()
        ag_copy(1).start()

    mate_copy(1 - c).start()
    mate_copy(3 - c).start()
    mate_arrival(c).wait_recv()
    mate_arrival(c + 2).wait_recv()

    @pl.when(c == 1)
    def _():
        ag_copy(0).start()
        ag_copy(1).start()

    @pl.when(special)
    def _():
        for i in range(2):
            for q in range(len(HELPERS)):
                relay_out(q, i).start()

    @pl.when(jnp.logical_not(special))
    def _():
        ag_copy(2).start()
        ag_copy(3).start()

    mate_copy(c).start()
    mate_copy(c + 2).start()

    wo_cp.start()
    res_cp.start()
    wo_rm = remote(wout.at[0, :, others], wo.at[heads:], wo_s.at[0], wo_r.at[0], mate)
    res_rm = remote(acts.at[0, :, others], res.at[c], wo_s.at[1], wo_r.at[1], mate)
    res_in = remote(acts.at[0, :, mine], res.at[1 - c], wo_s.at[1], wo_r.at[1], mate)
    wo_rm.start()
    res_rm.start()

    kall[cached:, :] = jnp.zeros((4 * rows, HD), BF16)
    vall[cached:, :] = jnp.zeros((4 * rows, HD), BF16)
    for cp in small:
        cp.wait()
    lane = lax.broadcasted_iota(jnp.int32, (rows, HD), 1)
    sign = jnp.where(lane < HD // 2, -1.0, 1.0).astype(F32)
    row = lax.broadcasted_iota(jnp.int32, (rows, HD), 0)

    def tables(k, _):
        rel, b = lax.div(k, 2), lax.rem(k, 2)
        side = hi + rel - 2 * hi * rel
        pos = bidx[0] * (4 * rows) + (2 * side + b) * rows + row
        angle = pos.astype(F32) * freq[...]
        turns = jnp.floor(angle * np.float32(1.0 / (2.0 * math.pi)) + 0.5)
        angle = ((angle - turns * TURN[0]) - turns * TURN[1]) - turns * TURN[2]
        ct[span(k * rows, rows), :] = jnp.cos(angle)
        st[span(k * rows, rows), :] = jnp.sin(angle) * sign
        return 0

    lax.fori_loop(0, 4, tables, 0)
    none = F32(-jnp.inf)
    own_first = jnp.where(hi == 0, F32(0.0), none)
    other_first = jnp.where(hi == 1, F32(0.0), none)
    key_id = lax.broadcasted_iota(jnp.int32, bias.shape, 1)
    bias[...] = jnp.where(key_id < cached, jnp.where(key_id < vlen[0], F32(0.0), none), own_first)

    def project(x, rel, start, count, tiles=(2, 0, 1)):
        for n in tiles:
            y = jnp.dot(x, wq[:, 2 * n * HD : 2 * (n + 1) * HD], preferred_element_type=F32)
            for i in range(count):
                tok = span(2 * rel * rows + (start + i) * part, part)
                key_at = span(cached + 2 * rel * rows + (start + i) * part, part)
                cos, sin = ct[tok, :], st[tok, :]
                yb = y[i * part : (i + 1) * part]

                def turned(v):
                    return (v * cos + pltpu.roll(v, HD // 2, 1) * sin).astype(BF16)

                if n < 2:
                    for k in range(2):
                        at = (2 * n + k) * part
                        qb[rel, start + i, at : at + part, :] = turned(yb[:, k * HD : (k + 1) * HD])
                else:
                    kall[key_at, :] = turned(yb[:, :HD])
                    vall[key_at, :] = yb[:, HD:].astype(BF16)

    factor = np.float32(math.log2(math.e) / math.sqrt(HD))
    nt = (((1,), (1,)), ((), ()))
    near = cached + 2 * rows

    def att_copy(rel, r):
        k = 4 * rel + r
        at = span(r * part, part)
        return remote(att.at[rel, at, :heads], att.at[rel, at, heads:], at_s.at[k], at_r.at[k], mate)

    def hand_over(rel, r, o):
        at = span(r * part, part)
        for k in range(GROUP):
            att[rel, at, k * HD : (k + 1) * HD] = o[k * part : (k + 1) * part]
        att_copy(rel, r).start()

    def causal(r):
        qid = lax.rem(lax.broadcasted_iota(jnp.int32, (GROUP * part, 1), 0), part) + r * part
        return lax.broadcasted_iota(jnp.int32, (1, 2 * rows), 1) <= qid

    def softmax(sa, sb):
        m = jnp.maximum(jnp.max(sa, -1, keepdims=True), jnp.max(sb, -1, keepdims=True))
        ea = jnp.exp2((sa - m) * factor)
        eb = jnp.exp2((sb - m) * factor)
        return m, ea.astype(BF16), eb.astype(BF16), jnp.sum(ea, -1, keepdims=True) + jnp.sum(eb, -1, keepdims=True)

    def attend(r, _=0):
        q = qb[1, r]
        sa = lax.dot_general(q, kall[:near], nt, preferred_element_type=F32) + bias[...]
        sb = lax.dot_general(q, kall[near:], nt, preferred_element_type=F32)
        sb = jnp.where(causal(r), sb, none)
        _, ea, eb, tot = softmax(sa, sb)
        o = jnp.dot(ea, vall[:near], preferred_element_type=F32)
        o = o + jnp.dot(eb, vall[near:], preferred_element_type=F32)
        hand_over(1, r, (o / tot).astype(BF16))
        return 0

    def own_begin(r, _):
        q = qb[0, r]
        sa = lax.dot_general(q, kall[:cached], nt, preferred_element_type=F32) + bias[:, :cached]
        sb = lax.dot_general(q, kall[cached:near], nt, preferred_element_type=F32)
        sb = jnp.where(causal(r), sb, none)
        m, ea, eb, tot = softmax(sa, sb)
        o = jnp.dot(ea, vall[:cached], preferred_element_type=F32)
        acc[r] = o + jnp.dot(eb, vall[cached:near], preferred_element_type=F32)
        top[r] = m
        total[r] = tot
        return 0

    def own_more(r, core):
        keys = slice(near + core * rows, near + (core + 1) * rows)
        sa = lax.dot_general(qb[0, r], kall[keys], nt, preferred_element_type=F32) + other_first
        m = jnp.maximum(top[r], jnp.max(sa, -1, keepdims=True))
        scale = jnp.exp2((top[r] - m) * factor)
        ea = jnp.exp2((sa - m) * factor)
        o = acc[r] * scale + jnp.dot(ea.astype(BF16), vall[keys], preferred_element_type=F32)
        return m, total[r] * scale + jnp.sum(ea, -1, keepdims=True), o

    def own_middle(r, _):
        m, tot, o = own_more(r, 0)
        acc[r] = o
        top[r] = m
        total[r] = tot
        return 0

    def own_end(r):
        _, tot, o = own_more(r, 1)
        hand_over(0, r, (o / tot).astype(BF16))

    def piece(f):
        return span(f * PIECE, PIECE)

    def sum_copy(f):
        return remote(snd.at[piece(f)], rcv.at[piece(f)], rs_s.at[f], rs_r.at[f], sum_dev)

    def base_copy(f):
        return remote(bsnd.at[piece(f)], brcv.at[piece(f)], bs_s.at[f], bs_r.at[f], base_dev)

    def other_output(b):
        for i in range(2):
            att_copy(1, 2 * b + i).wait_recv()
        at = pl.ds(b * rows, rows)
        x = att[1, at, :]
        tile = wide // 8
        for n in range(8):
            cols = slice(n * tile, (n + 1) * tile)
            snd[at, cols] = jnp.dot(x, wo[:, cols], preferred_element_type=F32).astype(BF16)

    def send_sums(r):
        for i in range(per):
            sum_copy(r * per + i).start()

    def own_output(b):
        for i in range(2):
            att_copy(0, 2 * b + i).wait_recv()
        at = pl.ds(b * rows, rows)
        x = att[0, at, :]
        tile = wide // 8
        for n in range(8):
            cols = slice(n * tile, (n + 1) * tile)
            y = jnp.dot(x, wo[:, cols], preferred_element_type=F32)
            base[at, cols] = y + res[b, :, cols].astype(F32)

        @pl.when(special)
        def _():
            bsnd[at, :] = base[at, :].astype(BF16)
            for i in range(2 * per):
                base_copy(2 * b * per + i).start()

    in_block = 2 * per

    def x_copy(f):
        b, k = lax.div(f, in_block), lax.rem(f, in_block)
        return remote(
            fin.at[piece(f)], out.at[0, piece(k), mine], x_s.at[f], x_r.at[c * in_block + k], (nxt, 2 * hi + b)
        )

    def finish(f, _):
        sum_copy(f).wait_recv()

        @pl.when(special)
        def _():
            base_copy(f).wait_recv()
            fin[piece(f), :] = (brcv[piece(f), :].astype(F32) + rcv[piece(f), :].astype(F32)).astype(BF16)

        @pl.when(jnp.logical_not(special))
        def _():
            fin[piece(f), :] = (base[piece(f), :] + rcv[piece(f), :].astype(F32)).astype(BF16)

        x_copy(f).start()
        return 0

    mate_arrival(1 - c).wait_recv()
    mate_arrival(3 - c).wait_recv()
    wq_cp.wait()
    project(nrm[0:2].reshape(2 * rows, dim), 0, 0, 4)
    k_cp.wait()
    v_cp.wait()
    lax.fori_loop(0, 4, own_begin, 0)
    wo_cp.wait()
    wo_rm.wait_recv()
    res_cp.wait()
    res_in.wait_recv()

    for j in range(2):
        arrived(j).wait_recv()
        passed_on(j, c).start()

    @pl.when(relays)
    def _():
        for i in range(2):
            relay_out(0, i).wait_recv()
            relay_in(i).start()

    for j in range(2):
        passed_on(j, 1 - c).wait_recv()
    project(nrm[2], 1, 0, 2)
    lax.fori_loop(0, 2, attend, 0)
    lax.fori_loop(0, 4, own_middle, 0)
    other_output(0)
    send_sums(0)
    send_sums(1)

    for i in range(2):

        @pl.when(special)
        def _():
            for q in range(len(HELPERS)):
                relay_arrival(q, i).wait_recv()

        @pl.when(jnp.logical_not(special))
        def _():
            arrived(2 + i).wait_recv()

        passed_on(2 + i, c).start()

    passed_on(2, 1 - c).wait_recv()
    passed_on(3, 1 - c).wait_recv()
    project(nrm[3], 1, 2, 2, (2,))
    own_end(0)
    own_end(1)
    project(nrm[3], 1, 2, 2, (0, 1))
    own_output(0)
    finish(0, 0)
    finish(1, 0)
    own_end(2)
    own_end(3)
    attend(2)
    finish(2, 0)
    own_output(1)
    attend(3)
    finish(3, 0)
    other_output(1)
    send_sums(2)
    send_sums(3)
    lax.fori_loop(4, pieces, finish, 0)

    for j in range(AG):
        if j < 2:
            ag_copy(j).wait_send()
        mate_copy(j).wait_send()
        passed_on(j, c).wait_send()

    @pl.when(special)
    def _():
        for i in range(2):
            for q in range(len(HELPERS)):
                relay_out(q, i).wait_send()

    @pl.when(jnp.logical_not(special))
    def _():
        ag_copy(2).wait_send()
        ag_copy(3).wait_send()

    @pl.when(relays)
    def _():
        for i in range(2):
            relay_in(i).wait_send()

    wo_rm.wait_send()
    res_rm.wait_send()
    for rel in range(2):
        for r in range(4):
            att_copy(rel, r).wait_send()

    def drain(f, _):
        sum_copy(f).wait_send()
        x_copy(f).wait_send()
        return 0

    lax.fori_loop(0, pieces, drain, 0)

    @pl.when(special)
    def _():
        def drain_base(f, _):
            base_copy(f).wait_send()
            return 0

        lax.fori_loop(0, pieces, drain_base, 0)

    def arrive(k, _):
        side, f = lax.div(k, in_block), lax.rem(k, in_block)
        cols = span(side * wide, wide)
        remote(fin.at[piece(f)], out.at[0, piece(f), cols], x_s.at[k], x_r.at[k], mate).wait_recv()
        return 0

    lax.fori_loop(0, 2 * in_block, arrive, 0)


def split_turn():
    whole, parts = 2.0 * math.pi, []
    for _ in range(2):
        scale = 2.0 ** (math.frexp(whole)[1] - 10)
        part = math.floor(whole / scale) * scale
        parts.append(np.float32(part))
        whole -= part
    return (*parts, np.float32(whole))


TURN = split_turn()


def body(sections, acts, norm_gain, w_qkv, w_out, kv_cache, block_index, valid_len):
    rows, dim = acts.shape[1:]
    wide = dim // 2
    cached = kv_cache.shape[1]
    width = w_qkv.shape[2]
    heads = w_out.shape[1]
    exponent = 2.0 * (np.arange(HD) % (HD // 2)) / HD
    freq = jnp.asarray(np.exp(-np.log(500000.0) * exponent).astype(np.float32)[None])
    step = rows // 2
    pieces = 2 * rows // PIECE
    keys = cached + 4 * rows
    dma = pltpu.SemaphoreType.DMA
    hbm = pl.BlockSpec(memory_space=pltpu.HBM)
    return pl.pallas_call(
        functools.partial(kernel, sections),
        out_shape=pltpu.VMEM((1, rows, dim), BF16),
        in_specs=[hbm] * 8,
        out_specs=pl.BlockSpec(memory_space=pltpu.VMEM),
        scratch_shapes=[
            pltpu.SMEM((1,), jnp.int32),
            pltpu.SMEM((1,), jnp.int32),
            pltpu.VMEM((1, HD), F32),
            pltpu.VMEM((rows, dim), BF16),
            pltpu.VMEM((1, dim), F32),
            pltpu.VMEM((4, rows, dim), BF16),
            pltpu.VMEM((dim, width), BF16),
            pltpu.VMEM((2 * heads, wide), BF16),
            pltpu.VMEM((keys, HD), BF16),
            pltpu.VMEM((keys, HD), BF16),
            pltpu.VMEM((1, cached + 2 * rows), F32),
            pltpu.VMEM((4 * rows, HD), F32),
            pltpu.VMEM((4 * rows, HD), F32),
            pltpu.VMEM((2, 4, GROUP * step, HD), BF16),
            pltpu.VMEM((4, GROUP * step, HD), F32),
            pltpu.VMEM((4, GROUP * step, 1), F32),
            pltpu.VMEM((4, GROUP * step, 1), F32),
            pltpu.VMEM((2, 2 * rows, 2 * heads), BF16),
            pltpu.VMEM((2, rows, wide), BF16),
            pltpu.VMEM((2 * rows, wide), F32),
            pltpu.VMEM((2 * rows, wide), BF16),
            pltpu.VMEM((2 * rows, wide), BF16),
            pltpu.VMEM((2 * rows, wide), BF16),
            pltpu.VMEM((2 * rows, wide), BF16),
            pltpu.VMEM((2 * rows, wide), BF16),
            pltpu.VMEM((2, rows // AG, dim // len(HELPERS)), BF16),
            dma((AG + 9,)),
            dma((AG,)), dma((AG,)), dma((AG,)), dma((AG,)), dma((AG,)), dma((AG,)),
            dma((2,)), dma((2,)), dma((8,)), dma((8,)),
            dma((pieces,)), dma((pieces,)), dma((pieces,)), dma((pieces,)), dma((pieces,)), dma((pieces,)),
            dma((2 * len(HELPERS),)), dma((2,)), dma((2,)), dma((2 * len(HELPERS),)),
        ],
        compiler_params=pltpu.CompilerParams(
            collective_id=0, has_side_effects=True, vmem_limit_bytes=56 * 2**20
        ),
    )(block_index, valid_len, freq, acts, norm_gain, w_qkv, w_out, kv_cache)

def solution(mesh):
    in_specs = (
        P("section", "tensor", None),
        P("section", None),
        P("section", None, "tensor"),
        P("section", "tensor", None),
        P("section", None, "tensor"),
        P("section"),
        P("section"),
    )
    out_specs = P("section", "tensor", None)
    return jax.shard_map(
        functools.partial(body, mesh.shape["section"]),
        mesh=mesh, in_specs=in_specs, out_specs=out_specs, check_vma=False,
    )
```
